32 devices in a mesh: batch: 16 (over z, x, core), tensor: 2 (over y).
Axes of the slice: x: 2, y: 2, z: 4, core: 2. Of those that a mesh axis runs over, the one named last changes fastest.
Arguments:
- qkv: bfloat16 [16, 1536, 3, 3072], P('batch', None, None, 'tensor'), may hold values from -18 to 18, as said below
- text_len: int32 [16], replicated, may hold values from 1 to 512, as said below
- step_idx: int32 [16], P('batch'), may hold values from 0 to 27, as said below
- latent: float32 [16, 1024, 64], P('batch', 'tensor'), may hold values from -8 to 8, as said below
- w_out: bfloat16 [3072, 64], replicated, may hold values from -0.109375 to 0.109375
Outputs:
- attn_text: bfloat16 [16, 512, 3072], P('batch', 'tensor')
- velocity: float32 [16, 1024, 64], P('batch', 'tensor')
- new_latent: float32 [16, 1024, 64], P('batch', 'tensor')
The draws below stay inside these ranges and needn't reach their ends.
Inputs may be any that keep to these rules, and one draw needn't show every extreme that they name: `qkv`: floats of queries, keys and values. `text_len`: copy 2i is a prompt's conditional copy and 2i+1 its unconditional copy. Every conditional copy has 128 or more text tokens and some has 512; every unconditional copy has 64 or fewer and some has exactly 64. `step_idx`: both copies of a prompt carry the same step. Both copies of a prompt carry the same latent.
All inputs are finite; a program needn't handle non-finite values.
Results may differ from the reference program's by a relative error of at most 0.0047.
Values may be sent and summed in bfloat16 or wider, within the bound.
A program may use at most 192 MiB of HBM per device.

```python
import jax
import jax.numpy as jnp
from jax import lax

HEADS = 24
HD = 128
D = 3072
LAT = 64
TXT = 512
IMG = 1024
NSTEPS = 28
SEQ = 1536
COPIES = 16


def draw_qkv(key, part):
    array_shape = (COPIES, SEQ, 3, D)
    base_key = jax.random.fold_in(key, 0)
    sample = jax.random.truncated_normal(base_key, -6.0, 6.0, array_shape, jnp.float32)
    return sample.astype(jnp.bfloat16)


def draw_text_len(key, part):
    long_key, short_key, chosen_key = jax.random.split(key, 3)
    copy_index = jnp.arange(COPIES)
    long_lengths = jax.random.randint(long_key, (COPIES,), TXT // 4, TXT + 1)
    short_lengths = jax.random.randint(short_key, (COPIES,), 1, TXT // 8 + 1)
    lengths = jnp.where(copy_index % 2 == 0, long_lengths, short_lengths)
    chosen = jax.random.randint(chosen_key, (), 0, COPIES // 2)
    lengths = jnp.where(copy_index == 2 * chosen, TXT, lengths)
    lengths = jnp.where(copy_index == 2 * chosen + 1, TXT // 8, lengths)
    return lengths.astype(jnp.int32)


def draw_step_idx(key, part):
    step_key, chosen_key = jax.random.split(key)
    prompts = COPIES // 2
    prompt_index = jnp.arange(prompts)
    steps_drawn = jax.random.randint(step_key, (prompts,), 0, NSTEPS)
    chosen = jax.random.randint(chosen_key, (), 0, prompts)
    steps_drawn = jnp.where(prompt_index == chosen, NSTEPS - 1, steps_drawn)
    steps_drawn = jnp.where(prompt_index == (chosen + 1) % prompts, 0, steps_drawn)
    return jnp.repeat(steps_drawn, 2).astype(jnp.int32)


def draw_latent(key, part):
    base_key = jax.random.fold_in(key, 0)
    prompts = COPIES // 2
    sample = jax.random.truncated_normal(base_key, -6.0, 6.0, (prompts, IMG, LAT), jnp.float32)
    return jnp.repeat(sample, 2, axis=0)


def normal_values(own_key, extent, width, bound, dtype=jnp.bfloat16):
    entries = width * jax.random.normal(own_key, extent, jnp.float32)
    return jnp.clip(entries, min=-bound, max=bound).astype(dtype)


def setup_inputs(seed: int = 0) -> dict:
    seeds = jax.random.split(jax.random.key(seed), 6)
    qkv = draw_qkv(jax.random.fold_in(seeds[5], 71), 0)
    text_len = draw_text_len(jax.random.fold_in(seeds[5], 71), 0)
    step_idx = draw_step_idx(jax.random.fold_in(seeds[5], 71), 0)
    latent = draw_latent(jax.random.fold_in(seeds[5], 71), 0)
    w_out = normal_values(seeds[4], (D, LAT), D ** -0.5, 0.109375)
    return {"qkv": qkv, "text_len": text_len, "step_idx": step_idx, "latent": latent, "w_out": w_out}


guidance_scale = 3.5
plan_shift = 3.0
norm_eps = 1e-06

def sigma_at(step_value):
    remain = 1.0 - step_value / NSTEPS
    return plan_shift * remain / (1.0 + (plan_shift - 1.0) * remain)

def attend_head(query_head, key_head, value_head, text_length):
    score_scale = HD ** (-0.5)
    scores = jnp.dot(query_head, key_head.T, preferred_element_type=jnp.float32) * score_scale
    column = jnp.arange(key_head.shape[0])
    valid = (column >= TXT) | (column < text_length)
    scores = jnp.where(valid[None, :], scores, -jnp.inf)
    row_max = lax.optimization_barrier(jnp.max(scores, axis=1, keepdims=True))
    weights = jnp.exp(scores - row_max)
    denominator = lax.optimization_barrier(jnp.sum(weights, axis=1, keepdims=True))
    summed = jnp.dot(weights.astype(jnp.bfloat16), value_head, preferred_element_type=jnp.float32)
    return (summed / denominator).astype(jnp.bfloat16)

def project(hidden_rows, w_out):
    hidden = hidden_rows.astype(jnp.float32)
    row_mean = lax.optimization_barrier(jnp.mean(hidden, axis=1, keepdims=True))
    row_meansq = lax.optimization_barrier(jnp.mean(hidden * hidden, axis=1, keepdims=True))
    product = jnp.dot(hidden_rows, w_out, preferred_element_type=jnp.float32)
    colsum = lax.optimization_barrier(jnp.sum(w_out.astype(jnp.float32), axis=0))[None, :]
    return (product - row_mean * colsum) * lax.rsqrt(row_meansq - row_mean * row_mean + norm_eps)

def reference(qkv, text_len, step_idx, latent, w_out):

    def one_copy(packed):
        block, text_length = packed
        per_head = block.reshape(SEQ, 3, HEADS, HD).transpose(1, 2, 0, 3)

        def head_step(triple):
            return attend_head(triple[0], triple[1], triple[2], text_length)
        heads_out = lax.map(head_step, (per_head[0], per_head[1], per_head[2]))
        joined = heads_out.transpose(1, 0, 2).reshape(SEQ, HEADS * HD)
        row_index = jnp.arange(TXT)
        text_part = jnp.where((row_index < text_length)[:, None], joined[:TXT], jnp.zeros((), jnp.bfloat16))
        return (text_part, project(joined[TXT:], w_out))
    attn_text, raw_all = lax.map(one_copy, (qkv, text_len))
    pairs = raw_all.reshape(COPIES // 2, 2, IMG, LAT)
    guided = pairs[:, 1] + guidance_scale * (pairs[:, 0] - pairs[:, 1])
    guided = jnp.repeat(guided, 2, axis=0)
    step_value = step_idx.astype(jnp.float32)
    step_delta = sigma_at(step_value + 1.0) - sigma_at(step_value)
    new_latent = latent + step_delta[:, None, None] * guided
    return (attn_text, guided, new_latent)
```

```python
import functools

import jax
import jax.numpy as jnp
from jax import lax
from jax.experimental import pallas as pl
from jax.experimental.pallas import tpu as pltpu
from jax.sharding import PartitionSpec as P

HD = 128
TXT = 512
NSTEPS = 28

guidance_scale = 3.5
plan_shift = 3.0
norm_eps = 1e-06

LOG2_SCALE = 1.4426950408889634 * HD ** (-0.5)
ROWS = 256
CONTRACT_LAST = (((1,), (1,)), ((), ()))


def sigma_at(step_value):
    remain = 1.0 - step_value / NSTEPS
    return plan_shift * remain / (1.0 + (plan_shift - 1.0) * remain)


def prepare_keys(text_length, k_ref, v_ref, kk, vv):
    seq = k_ref.shape[1]
    keys = k_ref[0]
    row = lax.broadcasted_iota(jnp.int32, (TXT, HD), 0)
    valid = row < text_length
    spare = jnp.broadcast_to(keys[TXT : TXT + 1].astype(jnp.float32), (TXT, HD))
    text_keys = jnp.where(valid, keys[:TXT].astype(jnp.float32), spare).astype(jnp.bfloat16)
    kk[:TXT, :HD] = text_keys
    kk[:TXT, HD:] = text_keys
    kk[TXT:, :HD] = keys[TXT:]
    kk[TXT:, HD:] = keys[TXT:]
    text_values = jnp.where(valid, v_ref[0, :TXT].astype(jnp.float32), 0.0)
    vv[:TXT, :HD] = text_values.astype(jnp.bfloat16)
    vv[:TXT, HD:] = jnp.where(valid, 1.0, 0.0).astype(jnp.bfloat16)
    vv[TXT:, :HD] = v_ref[0, TXT:]
    vv[TXT:, HD:] = jnp.ones((seq - TXT, HD), jnp.bfloat16)


def attend(query, kk, vv):
    scaled = query.astype(jnp.float32) * LOG2_SCALE
    high = scaled.astype(jnp.bfloat16)
    low = (scaled - high.astype(jnp.float32)).astype(jnp.bfloat16)
    both = jnp.concatenate([high, low], axis=1)
    scores = lax.dot_general(both, kk[...], CONTRACT_LAST, preferred_element_type=jnp.float32)
    row_max = jnp.max(scores, axis=1, keepdims=True)
    weights = jnp.exp2(scores - row_max).astype(jnp.bfloat16)
    summed = jnp.dot(weights, vv[...], preferred_element_type=jnp.float32)
    return (summed[:, :HD] / summed[:, HD:]).astype(jnp.bfloat16)


def text_kernel(length_ref, q_ref, k_ref, v_ref, out_ref, kk, vv):
    text_length = length_ref[0]
    prepare_keys(text_length, k_ref, v_ref, kk, vv)
    for start in range(0, TXT, ROWS):
        result = attend(q_ref[0, start : start + ROWS], kk, vv)
        row = start + lax.broadcasted_iota(jnp.int32, (ROWS, HD), 0)
        kept = jnp.where(row < text_length, result.astype(jnp.float32), 0.0)
        out_ref[start : start + ROWS, :] = kept.astype(jnp.bfloat16)


def image_kernel(length_ref, q_ref, k_ref, v_ref, w_ref, out_ref, kk, vv):
    image = out_ref.shape[1]

    @pl.when(pl.program_id(0) == 0)
    def _():
        out_ref[...] = jnp.zeros_like(out_ref)

    prepare_keys(length_ref[0], k_ref, v_ref, kk, vv)
    ones = jnp.ones((8, 2 * HD), jnp.bfloat16)
    for start in range(0, image, ROWS):
        result = attend(q_ref[0, TXT + start : TXT + start + ROWS], kk, vv)
        wide = result.astype(jnp.float32)
        square = wide * wide
        high = square.astype(jnp.bfloat16)
        low = (square - high.astype(jnp.float32)).astype(jnp.bfloat16)
        squares = jnp.concatenate([high, low], axis=1)
        span = slice(start, start + ROWS)
        out_ref[:72, span] += lax.dot_general(
            w_ref[...], result, CONTRACT_LAST, preferred_element_type=jnp.float32
        )
        out_ref[72:, span] += lax.dot_general(
            ones, squares, CONTRACT_LAST, preferred_element_type=jnp.float32
        )


def head_specs(seq):
    def part(which):
        return pl.BlockSpec((1, seq, HD), lambda h, length: (which, 0, h))

    return [part(0), part(1), part(2)]


def scratch(seq):
    return [pltpu.VMEM((seq, 2 * HD), jnp.bfloat16), pltpu.VMEM((seq, 2 * HD), jnp.bfloat16)]


def cost(heads, rows, seq):
    return pl.CostEstimate(
        flops=8 * heads * rows * seq * HD,
        bytes_accessed=6 * heads * seq * HD,
        transcendentals=heads * rows * seq,
    )


def attend_text(length, local):
    seq, width = local.shape[1:]
    heads = width // HD
    return pl.pallas_call(
        text_kernel,
        grid_spec=pltpu.PrefetchScalarGridSpec(
            num_scalar_prefetch=1,
            grid=(heads,),
            in_specs=head_specs(seq),
            out_specs=pl.BlockSpec((TXT, HD), lambda h, length: (0, h)),
            scratch_shapes=scratch(seq),
        ),
        out_shape=jax.ShapeDtypeStruct((TXT, width), jnp.bfloat16),
        compiler_params=pltpu.CompilerParams(vmem_limit_bytes=40 * 2**20),
        cost_estimate=cost(heads, TXT, seq),
    )(length, local, local, local)


def attend_image(length, local, weight):
    seq, width = local.shape[1:]
    heads = width // HD
    image = seq - TXT
    return pl.pallas_call(
        image_kernel,
        grid_spec=pltpu.PrefetchScalarGridSpec(
            num_scalar_prefetch=1,
            grid=(heads,),
            in_specs=head_specs(seq) + [pl.BlockSpec((72, HD), lambda h, length: (0, h))],
            out_specs=pl.BlockSpec((80, image), lambda h, length: (0, 0)),
            scratch_shapes=scratch(seq),
        ),
        out_shape=jax.ShapeDtypeStruct((80, image), jnp.float32),
        compiler_params=pltpu.CompilerParams(vmem_limit_bytes=40 * 2**20),
        cost_estimate=cost(heads, image, seq),
    )(length, local, local, local, weight)


def per_device(qkv, text_len, step_idx, latent, w_out):
    local = jnp.transpose(qkv[0], (1, 0, 2))
    width = local.shape[2]
    shares = lax.axis_size("tensor")
    position = lax.axis_index("batch")
    share = lax.axis_index("tensor")
    length = lax.dynamic_slice_in_dim(text_len, position, 1)

    text_out = attend_text(length, local)
    text_rows = TXT // shares
    if shares == 2:
        kept = lax.dynamic_slice_in_dim(text_out, share * text_rows, text_rows)
        sent = lax.dynamic_slice_in_dim(text_out, (1 - share) * text_rows, text_rows)
        came = lax.ppermute(sent, "tensor", [(0, 1), (1, 0)])
        first = share == 0
        text_tokens = jnp.concatenate(
            [jnp.where(first, kept, came), jnp.where(first, came, kept)], axis=1
        )
    else:
        text_tokens = lax.all_to_all(text_out, "tensor", split_axis=0, concat_axis=1, tiled=True)

    weight_t = jnp.transpose(w_out)
    own = lax.dynamic_slice_in_dim(weight_t, share * width, width, axis=1)
    own = jnp.concatenate([own, jnp.ones((8, width), jnp.bfloat16)], axis=0)
    sums = attend_image(length, local, own)
    sums = jnp.concatenate([sums[:65], sums[72:73]], axis=0)
    image_rows = sums.shape[1] // shares
    if shares == 2:
        kept = lax.dynamic_slice_in_dim(sums, share * image_rows, image_rows, axis=1)
        sent = lax.dynamic_slice_in_dim(sums, (1 - share) * image_rows, image_rows, axis=1)
        total = kept + lax.ppermute(sent, "tensor", [(0, 1), (1, 0)])
    else:
        total = lax.psum_scatter(sums, "tensor", scatter_dimension=1, tiled=True)

    depth = w_out.shape[0]
    colsum = jnp.sum(weight_t.astype(jnp.float32), axis=1, keepdims=True)
    row_mean = total[64:65] / depth
    row_meansq = total[65:66] / depth
    raw = (total[:64] - row_mean * colsum) * lax.rsqrt(row_meansq - row_mean * row_mean + norm_eps)
    pairs = [(source, source ^ 1) for source in range(lax.axis_size("batch"))]
    partner = lax.ppermute(raw.astype(jnp.bfloat16), "batch", pairs).astype(jnp.float32)
    is_cond = position % 2 == 0
    cond_velocity = jnp.where(is_cond, raw, partner)
    uncond_velocity = jnp.where(is_cond, partner, raw)
    guided = uncond_velocity + guidance_scale * (cond_velocity - uncond_velocity)
    step_value = step_idx[0].astype(jnp.float32)
    step_delta = sigma_at(step_value + 1.0) - sigma_at(step_value)
    updated = jnp.transpose(latent[0]) + step_delta * guided
    return (text_tokens[None], jnp.transpose(guided)[None], jnp.transpose(updated)[None])


def solution(mesh):
    placed = (P("batch", None, None, "tensor"), P(), P("batch"), P("batch", "tensor", None), P())
    return jax.shard_map(
        per_device,
        mesh=mesh,
        in_specs=placed,
        out_specs=(
            P("batch", "tensor", None),
            P("batch", "tensor", None),
            P("batch", "tensor", None),
        ),
        check_vma=False,
    )
```

```python
import functools

import jax
import jax.numpy as jnp
from jax import lax
from jax.experimental import pallas as pl
from jax.experimental.pallas import tpu as pltpu
from jax.sharding import PartitionSpec as P

HD = 128
TXT = 512
NSTEPS = 28

guidance_scale = 3.5
plan_shift = 3.0
norm_eps = 1e-06

LOG2_SCALE = 1.4426950408889634 * HD ** (-0.5)
ROWS = 256
CONTRACT_LAST = (((1,), (1,)), ((), ()))


def sigma_at(step_value):
    remain = 1.0 - step_value / NSTEPS
    return plan_shift * remain / (1.0 + (plan_shift - 1.0) * remain)


def prepare_keys(text_length, k_ref, v_ref, kk, vv):
    seq = k_ref.shape[1]
    keys = k_ref[0]
    row = lax.broadcasted_iota(jnp.int32, (TXT, HD), 0)
    valid = row < text_length
    spare = jnp.broadcast_to(keys[TXT : TXT + 1].astype(jnp.float32), (TXT, HD))
    text_keys = jnp.where(valid, keys[:TXT].astype(jnp.float32), spare).astype(jnp.bfloat16)
    kk[:TXT, :HD] = text_keys
    kk[:TXT, HD:] = text_keys
    kk[TXT:, :HD] = keys[TXT:]
    kk[TXT:, HD:] = keys[TXT:]
    text_values = jnp.where(valid, v_ref[0, :TXT].astype(jnp.float32), 0.0)
    vv[:TXT, :HD] = text_values.astype(jnp.bfloat16)
    vv[:TXT, HD:] = jnp.where(valid, 1.0, 0.0).astype(jnp.bfloat16)
    vv[TXT:, :HD] = v_ref[0, TXT:]
    vv[TXT:, HD:] = jnp.ones((seq - TXT, HD), jnp.bfloat16)


def score_block(query, kk):
    scaled = query.astype(jnp.float32) * LOG2_SCALE
    high = scaled.astype(jnp.bfloat16)
    low = (scaled - high.astype(jnp.float32)).astype(jnp.bfloat16)
    both = jnp.concatenate([high, low], axis=1)
    return lax.dot_general(both, kk[...], CONTRACT_LAST, preferred_element_type=jnp.float32)


def weigh(scores, vv):
    row_max = jnp.max(scores, axis=1, keepdims=True)
    weights = jnp.exp2(scores - row_max).astype(jnp.bfloat16)
    summed = jnp.dot(weights, vv[...], preferred_element_type=jnp.float32)
    return (summed[:, :HD] / summed[:, HD:]).astype(jnp.bfloat16)


def attend_group(text_length, q_ref, k_ref, v_ref, kk, vv, first, count, finish):
    heads = q_ref.shape[2] // HD
    tasks = [(h, r) for h in range(heads) for r in range(0, count, ROWS)]

    def scores_of(task):
        head, row = task
        lanes = pl.ds(head * HD, HD)
        if row == 0:
            prepare_keys(
                text_length,
                k_ref.at[:, :, lanes],
                v_ref.at[:, :, lanes],
                kk.at[head],
                vv.at[head],
            )
        return score_block(q_ref[0, first + row : first + row + ROWS, lanes], kk.at[head])

    scores = scores_of(tasks[0])
    for index, (head, row) in enumerate(tasks):
        later = scores_of(tasks[index + 1]) if index + 1 < len(tasks) else None
        finish(head, row, weigh(scores, vv.at[head]))
        scores = later


def text_kernel(length_ref, q_ref, k_ref, v_ref, out_ref, kk, vv):
    text_length = length_ref[lax.axis_index("batch")]

    def finish(head, row, result):
        place = row + lax.broadcasted_iota(jnp.int32, (ROWS, HD), 0)
        kept = jnp.where(place < text_length, result.astype(jnp.float32), 0.0)
        out_ref[row : row + ROWS, head * HD : (head + 1) * HD] = kept.astype(jnp.bfloat16)

    attend_group(text_length, q_ref, k_ref, v_ref, kk, vv, 0, TXT, finish)


def image_kernel(length_ref, q_ref, k_ref, v_ref, w_ref, out_ref, col_ref, kk, vv, held):
    image = out_ref.shape[1]
    steps, _, group = held.shape
    width = steps * group
    step = pl.program_id(0)

    def finish(head, row, result):
        held[step, row : row + ROWS, head * HD : (head + 1) * HD] = result

    text_length = length_ref[lax.axis_index("batch")]
    attend_group(text_length, q_ref, k_ref, v_ref, kk, vv, TXT, image, finish)

    @pl.when(step == steps - 1)
    def _():
        total = jnp.sum(w_ref[...].astype(jnp.float32), axis=1, keepdims=True)
        col_ref[...] = jnp.broadcast_to(total, col_ref.shape)
        start = pl.multiple_of(lax.axis_index("tensor") * width, HD)
        own = w_ref[:, pl.ds(start, width)]
        own = jnp.concatenate([own, jnp.ones((8, width), jnp.bfloat16)], axis=0)
        for row in range(0, image, ROWS):
            span = slice(row, row + ROWS)
            product = jnp.zeros((72, ROWS), jnp.float32)
            square = jnp.zeros((ROWS, HD), jnp.float32)
            for part in range(steps):
                tokens = held[part, span, :]
                product += lax.dot_general(
                    own[:, part * group : (part + 1) * group],
                    tokens,
                    CONTRACT_LAST,
                    preferred_element_type=jnp.float32,
                )
                for lane in range(0, group, HD):
                    wide = tokens[:, lane : lane + HD].astype(jnp.float32)
                    square += wide * wide
            out_ref[:72, span] = product
            squares = jnp.sum(jnp.transpose(square), axis=0, keepdims=True)
            out_ref[72:, span] = jnp.broadcast_to(squares, (8, ROWS))


def grouping(width):
    heads = width // HD
    together = 3 if heads % 3 == 0 else 1
    return heads // together, together * HD


def head_specs(seq, group):
    def part(which):
        return pl.BlockSpec((1, seq, group), lambda h, length: (which, 0, h))

    return [part(0), part(1), part(2)]


def scratch(seq, group):
    shape = (group // HD, seq, 2 * HD)
    return [pltpu.VMEM(shape, jnp.bfloat16), pltpu.VMEM(shape, jnp.bfloat16)]


def cost(width, rows, seq):
    return pl.CostEstimate(
        flops=8 * rows * seq * width,
        bytes_accessed=6 * seq * width,
        transcendentals=width // HD * rows * seq,
    )


def attend_text(lengths, local):
    seq, width = local.shape[1:]
    steps, group = grouping(width)
    return pl.pallas_call(
        text_kernel,
        grid_spec=pltpu.PrefetchScalarGridSpec(
            num_scalar_prefetch=1,
            grid=(steps,),
            in_specs=head_specs(seq, group),
            out_specs=pl.BlockSpec((TXT, group), lambda h, length: (0, h)),
            scratch_shapes=scratch(seq, group),
        ),
        out_shape=jax.ShapeDtypeStruct((TXT, width), jnp.bfloat16),
        compiler_params=pltpu.CompilerParams(vmem_limit_bytes=48 * 2**20),
        cost_estimate=cost(width, TXT, seq),
    )(lengths, local, local, local)


def attend_image(lengths, local, weight):
    seq, width = local.shape[1:]
    steps, group = grouping(width)
    image = seq - TXT
    lanes, depth = weight.shape
    return pl.pallas_call(
        image_kernel,
        grid_spec=pltpu.PrefetchScalarGridSpec(
            num_scalar_prefetch=1,
            grid=(steps,),
            in_specs=head_specs(seq, group)
            + [pl.BlockSpec((lanes, depth), lambda h, length: (0, 0))],
            out_specs=[
                pl.BlockSpec((80, image), lambda h, length: (0, 0)),
                pl.BlockSpec((lanes, HD), lambda h, length: (0, 0)),
            ],
            scratch_shapes=scratch(seq, group) + [pltpu.VMEM((steps, image, group), jnp.bfloat16)],
        ),
        out_shape=[
            jax.ShapeDtypeStruct((80, image), jnp.float32),
            jax.ShapeDtypeStruct((lanes, HD), jnp.float32),
        ],
        compiler_params=pltpu.CompilerParams(vmem_limit_bytes=48 * 2**20),
        cost_estimate=cost(width, image, seq),
    )(lengths, local, local, local, weight)


def per_device(qkv, text_len, step_idx, latent, w_out):
    local = jnp.transpose(qkv[0], (1, 0, 2))
    shares = lax.axis_size("tensor")
    position = lax.axis_index("batch")
    share = lax.axis_index("tensor")

    text_out = attend_text(text_len, local)
    text_rows = TXT // shares
    if shares == 2:
        text_kept = lax.dynamic_slice_in_dim(text_out, share * text_rows, text_rows)
        sent = lax.dynamic_slice_in_dim(text_out, (1 - share) * text_rows, text_rows)
        text_came = lax.ppermute(sent, "tensor", [(0, 1), (1, 0)])
    else:
        text_tokens = lax.all_to_all(text_out, "tensor", split_axis=0, concat_axis=1, tiled=True)

    weight_t = jnp.transpose(w_out)
    weight_t, text_out = lax.optimization_barrier((weight_t, text_out))
    sums, colsum = attend_image(text_len, local, weight_t)
    sums = jnp.concatenate([sums[:65], sums[72:73]], axis=0)
    if shares == 2:
        sums, came = lax.optimization_barrier((sums, text_came))
        first = share == 0
        text_tokens = jnp.concatenate(
            [jnp.where(first, text_kept, came), jnp.where(first, came, text_kept)], axis=1
        )
    image_rows = sums.shape[1] // shares
    if shares == 2:
        kept = lax.dynamic_slice_in_dim(sums, share * image_rows, image_rows, axis=1)
        sent = lax.dynamic_slice_in_dim(sums, (1 - share) * image_rows, image_rows, axis=1)
        total = kept + lax.ppermute(sent, "tensor", [(0, 1), (1, 0)])
    else:
        total = lax.psum_scatter(sums, "tensor", scatter_dimension=1, tiled=True)

    depth = w_out.shape[0]
    colsum = colsum[:, :1]
    row_mean = total[64:65] / depth
    row_meansq = total[65:66] / depth
    raw = (total[:64] - row_mean * colsum) * lax.rsqrt(row_meansq - row_mean * row_mean + norm_eps)
    pairs = [(source, source ^ 1) for source in range(lax.axis_size("batch"))]
    partner = lax.ppermute(raw.astype(jnp.bfloat16), "batch", pairs).astype(jnp.float32)
    is_cond = position % 2 == 0
    cond_velocity = jnp.where(is_cond, raw, partner)
    uncond_velocity = jnp.where(is_cond, partner, raw)
    guided = uncond_velocity + guidance_scale * (cond_velocity - uncond_velocity)
    step_value = step_idx[0].astype(jnp.float32)
    step_delta = sigma_at(step_value + 1.0) - sigma_at(step_value)
    updated = jnp.transpose(latent[0]) + step_delta * guided
    return (text_tokens[None], jnp.transpose(guided)[None], jnp.transpose(updated)[None])


def solution(mesh):
    placed = (P("batch", None, None, "tensor"), P(), P("batch"), P("batch", "tensor", None), P())
    return jax.shard_map(
        per_device,
        mesh=mesh,
        in_specs=placed,
        out_specs=(
            P("batch", "tensor", None),
            P("batch", "tensor", None),
            P("batch", "tensor", None),
        ),
        check_vma=False,
    )
```
